512 devices in a mesh: batch: 64 (over z_lo, x, y), param: 8 (over z_hi, core).
Axes of the slice: x: 4, y: 8, z: 8 (z_hi: 4, z_lo: 2; z = z_hi * 2 + z_lo), core: 2. Of those that a mesh axis runs over, the one named last changes fastest.
Arguments:
- target_backbone_features: bfloat16 [4096, 2048], P(('batch', 'param')), may hold values from -6 to 6
- closing_layernorm_gain: float32 [2048], replicated, may hold values from 0.5 to 1.5
- projection_weights_table: bfloat16 [2048, 1024], P('batch', 'param'), may hold values from -0.125 to 0.125
- source_raw_vectors: bfloat16 [32768, 1024], P(('batch', 'param')), may hold values from -0.5 to 0.5
- matching_target_ids: int32 [32768], P(('batch', 'param')), may hold values from 0 to 4095
- sharpness_parameter: float32 [1], replicated, may hold values from 5 to 15
- similarity_shift_term: float32 [1], replicated, may hold values from -4 to -2
Outputs:
- state_grad: bfloat16 [32768, 1024], P(('batch', 'param'))
- head_grad: float32 [2048, 1024], P('batch', 'param')
The draws below stay inside these ranges and needn't reach their ends.
All inputs are finite; a program needn't handle non-finite values.
Results may differ from the reference program's by a relative error of at most 0.02.
Values may be sent and summed in bfloat16 or wider, within the bound.
A program may use at most 64 MiB of HBM per device.

```python
import math
import jax
import jax.numpy as jnp
from jax import lax

D = 2048
E = 1024
G_DEV = 8
NG = 4096
NS = 32768
N_PARAM = 8


def place_ends(values, key, low, top_value):
    longest = values.shape.index(max(values.shape))
    spots = []
    for shift in (0, 1):
        where = [jax.random.randint(jax.random.fold_in(key, axis), (), 0, length) for axis, length in enumerate(values.shape)]
        where[longest] = (where[longest] + shift) % values.shape[longest]
        spots.append(tuple(where))
    return values.at[spots[0]].set(low).at[spots[1]].set(top_value)


def block_scale(key, extent, cuts, smallest, high):
    def one(dim, shards_of):
        heights = jax.random.uniform(jax.random.fold_in(jax.random.fold_in(key, 6), dim), (shards_of,), jnp.float32, smallest / len(cuts), high / len(cuts))
        return jnp.repeat(jnp.exp(heights), extent[dim] // shards_of).reshape((-1,) + (1,) * (len(extent) - dim - 1))

    level = one(*cuts[0])
    for cut in cuts[1:]:
        level = level * one(*cut)
    return level


def bell_draw(own_key, shape, spread, reach, split=(), held_as=jnp.bfloat16):
    entries = jax.random.normal(own_key, shape, jnp.float32) * spread
    if len(split) > 0:
        entries = block_scale(own_key, shape, split, -0.22, 0.18) * entries
    return jnp.clip(entries, min=-reach, max=reach).astype(held_as)


def setup_inputs(seed: int = 0) -> dict:
    key_list = jax.random.split(jax.random.key(seed), 8)
    return {
        "target_backbone_features": bell_draw(key_list[0], (NG, D), 1.0, 6.0, ((0, 512),)),
        "closing_layernorm_gain": jnp.clip(1.0 + 0.1 * jax.random.normal(key_list[1], (D,), jnp.float32), 0.5, 1.5),
        "projection_weights_table": bell_draw(key_list[2], (D, E), D ** -0.5, 0.125, ((0, 64), (1, 8))),
        "source_raw_vectors": bell_draw(key_list[3], (NS, E), 0.03125, 0.5, ((0, 512),)),
        "matching_target_ids": place_ends(jax.random.randint(key_list[4], (NS,), 0, NG), jax.random.fold_in(key_list[4], 1), 0, NG - 1).astype(jnp.int32),
        "sharpness_parameter": jnp.clip(jnp.exp(jax.random.uniform(key_list[5], (1,), jnp.float32, math.log(5.0), math.log(15.0))), 5.0, 15.0),
        "similarity_shift_term": jnp.clip(jax.random.uniform(key_list[6], (1,), jnp.float32, -4.0, -2.0), -4.0, -2.0),
    }


def reference(target_backbone_features, closing_layernorm_gain, projection_weights_table, source_raw_vectors, matching_target_ids, sharpness_parameter, similarity_shift_term):
    features = target_backbone_features.astype(jnp.float32)
    scaled = lax.rsqrt(lax.optimization_barrier(jnp.mean(features * features, axis=1, keepdims=True)) + 1e-06)
    normed = (features * scaled * closing_layernorm_gain).astype(jnp.bfloat16)
    raw = jnp.dot(normed, projection_weights_table, preferred_element_type=jnp.float32).astype(jnp.bfloat16)
    raw_f = raw.astype(jnp.float32)
    goal_scale = lax.rsqrt(lax.optimization_barrier(jnp.sum(raw_f * raw_f, axis=1, keepdims=True)) + 1e-06)
    goal_unit_f = raw_f * goal_scale
    target_normalized_vectors = goal_unit_f.astype(jnp.bfloat16)
    state_f = source_raw_vectors.astype(jnp.float32)
    state_inverse_norm = lax.rsqrt(lax.optimization_barrier(jnp.sum(state_f * state_f, axis=1, keepdims=True)) + 1e-06)
    state_unit_f = state_f * state_inverse_norm
    state_unit_embedding = state_unit_f.astype(jnp.bfloat16)
    sharpness_multiplier = sharpness_parameter[0]
    shift_amount_value = similarity_shift_term[0]
    block_rows = 512 if NS % 512 == 0 else NS
    block_count = NS // block_rows
    group_blocks = NG // (G_DEV * N_PARAM)
    grouped = target_normalized_vectors.astype(jnp.float32).reshape(group_blocks, N_PARAM, G_DEV, E)
    goal_row_index = jnp.arange(NG, dtype=jnp.int32)

    def one_block(carry, inputs):
        normalized_source_vectors, pos_rows = inputs
        pair_similarity_scores = sharpness_multiplier * jnp.dot(normalized_source_vectors, target_normalized_vectors.T, preferred_element_type=jnp.float32) + shift_amount_value
        label_polarity = jnp.where(pos_rows[:, None] == goal_row_index[None, :], 1.0, -1.0).astype(jnp.float32)
        coupling_coefficient = (-sharpness_multiplier * label_polarity * jax.nn.sigmoid(-label_polarity * pair_similarity_scores)).astype(jnp.bfloat16)
        weight_f = coupling_coefficient.astype(jnp.float32).reshape(block_rows, group_blocks, N_PARAM, G_DEV)
        partials = jnp.einsum('rkqc,kqce->qre', weight_f, grouped)
        rounded = lax.optimization_barrier(partials.astype(jnp.bfloat16))
        unit_grad = lax.optimization_barrier(jnp.sum(rounded.astype(jnp.float32), axis=0))
        carry = carry + jnp.dot(coupling_coefficient.T, normalized_source_vectors, preferred_element_type=jnp.float32)
        return (carry, unit_grad)
    start = jnp.zeros((NG, E), jnp.float32)
    unit_goal_grad, unit_blocks = lax.scan(one_block, start, (state_unit_embedding.reshape(block_count, block_rows, E), matching_target_ids.reshape(block_count, block_rows)))
    unit_state_grad = unit_blocks.reshape(NS, E)
    inner_s = lax.optimization_barrier(jnp.sum(state_unit_f * unit_state_grad, axis=1, keepdims=True))
    state_grad = (state_inverse_norm * (unit_state_grad - state_unit_f * inner_s)).astype(jnp.bfloat16)
    inner_g = lax.optimization_barrier(jnp.sum(goal_unit_f * unit_goal_grad, axis=1, keepdims=True))
    raw_grad = (goal_scale * (unit_goal_grad - goal_unit_f * inner_g)).astype(jnp.bfloat16)
    head_grad = jnp.dot(normed.T, raw_grad, preferred_element_type=jnp.float32)
    return (state_grad, head_grad)
```

```python
import jax
import jax.numpy as jnp
from jax import lax
from jax.experimental import pallas as pl
from jax.experimental.pallas import tpu as pltpu
from jax.sharding import PartitionSpec as P

F32 = jnp.float32
BF16 = jnp.bfloat16
MESH = pl.DeviceIdType.MESH
NX, NY, NZ = 4, 8, 8
N_SEM = 160
FAR_Y = (4, 3, 5, 2, 6, 1, 7)
FAR_X = (2, 1, 3)


def dot(a, b, contract=((1,), (0,))):
    return lax.dot_general(a, b, (contract, ((), ())), preferred_element_type=F32)


def kernel(
    feat, gain, wblk, src, idrow, sharp, shift,
    sg_out, hg_out,
    nbuf, wbuf, rpart, rbuf, gown, gbuf, sbuf, idbuf, pt,
    uown, usend, urecv, ub, ua1, ub1, ta, tb, ua2, ub2, xbuf,
    rgb, rgr, hbuf, ha1, hb1, hta, htb, ha2, hb2, hz, hzr,
    spbuf, srecv, send_sem, recv_sem,
):
    b = lax.axis_index("batch")
    p = lax.axis_index("param")
    zlo = b // 32
    x = lax.rem(b // 8, NX)
    y = lax.rem(b, NY)
    zhi = p // 2
    core = lax.rem(p, 2)
    z = zhi * 2 + zlo

    def dev(x=x, y=y, z=z, core=core):
        return (lax.rem(z, 2) * 32 + x * 8 + y, (z // 2) * 2 + core)

    def xd(d):
        return lax.rem(x + d, NX)

    def yd(d):
        return lax.rem(y + d, NY)

    def zd(d):
        return lax.rem(z + d, NZ)

    peers = [dev(y=yd(d)) for d in range(1, NY)]
    peers += [dev(x=xd(d)) for d in range(1, NX)]
    peers += [dev(z=zd(d)) for d in range(1, NZ)]
    peers += [dev(z=zd(d), core=1 - core) for d in (0, 2, 4, 6)]
    barrier = pltpu.get_barrier_semaphore()
    for peer in peers:
        pl.semaphore_signal(barrier, inc=1, device_id=peer, device_id_type=MESH)

    f = feat[...].astype(F32)
    nf = f * lax.rsqrt(jnp.mean(f * f, axis=1, keepdims=True) + 1e-6) * gain[...]
    nbuf[zhi, core] = jnp.concatenate([nf[:, :1024], nf[:, 1024:]], axis=0).astype(BF16)
    wbuf[x, y, pl.ds(pl.multiple_of(zlo * 32, 32), 32), :] = wblk[...]
    idbuf[z] = idrow[...]
    s_f = src[...].astype(F32)
    s_scale = lax.rsqrt(jnp.sum(s_f * s_f, axis=1, keepdims=True) + 1e-6)
    s_unit = (s_f * s_scale).astype(BF16)
    sbuf[0, z] = s_unit[:, :512]
    sbuf[1, z] = s_unit[:, 512:]

    pl.semaphore_wait(barrier, len(peers))

    started = []

    def cp(a, c, device):
        i = len(started)
        copy = pltpu.make_async_remote_copy(
            src_ref=a, dst_ref=c, send_sem=send_sem.at[i], recv_sem=recv_sem.at[i],
            device_id=device, device_id_type=MESH,
        )
        copy.start()
        started.append(copy)
        return copy

    def arrived(copies):
        for copy in copies:
            copy.wait_recv()

    def over_x(src_of, dst_of):
        return [cp(src_of(xd(d)), dst_of(d), dev(x=xd(d))) for d in FAR_X]

    def over_y(src_of, dst_of):
        return [cp(src_of(yd(d)), dst_of(d), dev(y=yd(d))) for d in FAR_Y]

    wz = wbuf.at[x, y, pl.ds(pl.multiple_of(zlo * 32, 32), 32), :]
    c_wz = cp(wz, wz, dev(z=z + 1 - 2 * zlo))
    c_n = [cp(nbuf.at[zhi, core], nbuf.at[zhi, core], dev(z=zd(d))) for d in (4, 2, 6)]
    c_wz.wait_recv()
    wa, wb = pl.ds(0, 16), pl.ds(16, 48)
    w1a = over_x(lambda t: wbuf.at[x, y, wa], lambda d: wbuf.at[x, y, wa])
    w1b = over_y(lambda t: wbuf.at[x, y, wb], lambda d: wbuf.at[x, y, wb])

    def hop(block, rows, step):
        ref = sbuf.at[:, block, rows]
        return cp(ref, ref, dev(z=zd(step)))

    every, low, high = pl.ds(0, 64), pl.ds(0, 32), pl.ds(32, 32)
    s_up, s_down = hop(z, every, 1), hop(z, every, 7)
    c_id = [cp(idbuf.at[z], idbuf.at[z], dev(z=zd(d))) for d in range(1, NZ)]

    arrived(w1a)
    w2a = over_y(lambda t: wbuf.at[:, y, wa], lambda d: wbuf.at[:, y, wa])
    arrived(w1b)
    w2b = over_x(lambda t: wbuf.at[x, :, wb], lambda d: wbuf.at[x, :, wb])
    arrived(c_n)
    c_ns = cp(nbuf.at[:, core], nbuf.at[:, core], dev(core=1 - core))
    s_up.wait_recv()
    s_down.wait_recv()
    s_up, s_down = hop(zd(7), every, 1), hop(zd(1), every, 7)
    c_ns.wait_recv()
    arrived(w2a)
    arrived(w2b)

    normed = nbuf[...].reshape(128, 1024)
    top = dot(normed, wbuf[:, :, 0:32, :].reshape(1024, 128)).reshape(8, 16, 128)
    bottom = dot(normed, wbuf[:, :, 32:64, :].reshape(1024, 128)).reshape(8, 16, 128)
    rpart[...] = (top[:, 0:8] + bottom[:, 8:16]).reshape(4, 16, 128).astype(BF16)
    rbuf[p] = rpart[zhi]
    c_r = []
    for d in (4, 2, 6, 0):
        to = zd(d)
        if d:
            c_r.append(cp(rpart.at[to // 2], rbuf.at[p], dev(z=to)))
        c_r.append(cp(rpart.at[to // 2], rbuf.at[p], dev(z=to, core=1 - core)))
    arrived(c_r)

    raw_f = jnp.concatenate([rbuf[k] for k in range(8)], axis=1).astype(F32)
    g_scale = lax.rsqrt(jnp.sum(raw_f * raw_f, axis=1, keepdims=True) + 1e-6)
    g_unit = (raw_f * g_scale).astype(BF16)
    gown[0] = g_unit[:, :512]
    gown[1] = g_unit[:, 512:]
    gbuf[core, x, y] = gown[core]
    ga, gb = pl.ds(0, 128), pl.ds(128, 384)
    g1a = over_x(lambda t: gbuf.at[core, x, y, :, ga], lambda d: gbuf.at[core, x, y, :, ga])
    g1b = over_y(lambda t: gbuf.at[core, x, y, :, gb], lambda d: gbuf.at[core, x, y, :, gb])
    s_up.wait_recv()
    s_down.wait_recv()
    s_up, s_down = hop(zd(6), every, 1), hop(zd(2), every, 7)
    arrived(g1a)
    g2a = over_y(lambda t: gbuf.at[core, :, y, :, ga], lambda d: gbuf.at[core, :, y, :, ga])
    arrived(g1b)
    g2b = over_x(lambda t: gbuf.at[core, x, :, :, gb], lambda d: gbuf.at[core, x, :, :, gb])
    s_up.wait_recv()
    s_down.wait_recv()
    s_up, s_down = hop(zd(5), low, 1), hop(zd(3), high, 7)
    arrived(g2a)
    arrived(g2b)
    c_g = cp(gbuf.at[core], gbuf.at[core], dev(core=1 - core))
    arrived(c_id)
    s_up.wait_recv()
    s_down.wait_recv()
    c_g.wait_recv()

    scale, offset = sharp[0], shift[0]
    ids = jnp.concatenate(
        [idbuf[2 * q, 0:1] + idbuf[2 * q + 1, 0:1] for q in range(4)], axis=1
    )
    row = lax.broadcasted_iota(jnp.int32, (128, 1), 0)

    def goals_step(k, carry):
        s0 = sbuf[0].reshape(512, 512)
        s1 = sbuf[1].reshape(512, 512)
        nt = ((1,), (1,))
        sim = dot(gbuf[0, k].reshape(128, 512), s0, nt) + dot(gbuf[1, k].reshape(128, 512), s1, nt)
        logits = scale * sim + offset
        goal = (lax.rem(z, 2) * 32 + k * 8 + row // 16) * 64 + zhi * 16 + lax.rem(row, 16)
        sign = jnp.where(goal == ids, 1.0, -1.0).astype(F32)
        weight = (-scale * sign / (1.0 + jnp.exp(sign * logits))).astype(BF16)
        pt[pl.ds(pl.multiple_of(k * 128, 128), 128), :] = weight
        uown[k] = dot(weight, sbuf[core].reshape(512, 512)).reshape(8, 16, 512)
        usend[k] = dot(weight, sbuf[1 - core].reshape(512, 512)).reshape(8, 16, 512).astype(BF16)
        return carry

    lax.fori_loop(0, NX, goals_step, 0)
    c_u = cp(usend, urecv, dev(core=1 - core))

    for q in range(4):
        lhs = pt[:, q * 128:(q + 1) * 128]
        for h in range(2):
            part = dot(lhs, gbuf[h].reshape(512, 512), ((0,), (0,)))
            spbuf[2 * q:2 * q + 2, h] = part.reshape(2, 64, 512).astype(BF16)

    c_u.wait_recv()
    for k in range(NX):
        ub[k] = (uown[k] + urecv[k].astype(F32)).astype(BF16)
    u1a = over_y(lambda t: ub.at[:, t, :, ga], lambda d: ua1.at[d - 1])
    u1b = over_x(lambda t: ub.at[t, :, :, gb], lambda d: ub1.at[d - 1])
    c_s = [cp(spbuf.at[zd(d)], srecv.at[d - 1], dev(z=zd(d))) for d in (4, 3, 5, 2, 6, 1, 7)]
    arrived(u1a)
    ta[...] = (ub[:, y, :, 0:128].astype(F32) + jnp.sum(ua1[...].astype(F32), axis=0)).astype(BF16)
    u2a = over_x(lambda t: ta.at[t], lambda d: ua2.at[d - 1])
    arrived(u1b)
    tb[...] = (ub[x, :, :, 128:512].astype(F32) + jnp.sum(ub1[...].astype(F32), axis=0)).astype(BF16)
    u2b = over_y(lambda t: tb.at[t], lambda d: ub2.at[d - 1])
    arrived(u2a)
    xbuf[core, :, 0:128] = ta[x].astype(F32) + jnp.sum(ua2[...].astype(F32), axis=0)
    arrived(u2b)
    xbuf[core, :, 128:512] = tb[y].astype(F32) + jnp.sum(ub2[...].astype(F32), axis=0)
    c_x = cp(xbuf.at[core], xbuf.at[core], dev(core=1 - core))
    c_x.wait_recv()

    u = jnp.concatenate([xbuf[0], xbuf[1]], axis=1)
    g_f = raw_f * g_scale
    inner = jnp.sum(g_f * u, axis=1, keepdims=True)
    raw_grad = (g_scale * (u - g_f * inner)).astype(BF16)
    for k in range(8):
        rgb[k] = raw_grad[:, k * 128:(k + 1) * 128]
    rgr[zhi] = rgb[p]
    c_rg = [cp(rgb.at[(zd(d) // 2) * 2 + core], rgr.at[zhi], dev(z=zd(d))) for d in (4, 2, 6)]
    arrived(c_rg)
    rg = rgr[...].astype(F32).reshape(8, 8, 128)
    zero = jnp.zeros((8, 8, 128), F32)
    rg_top = jnp.concatenate([rg, zero], axis=1).reshape(128, 128).astype(BF16)
    rg_bottom = jnp.concatenate([zero, rg], axis=1).reshape(128, 128).astype(BF16)
    normed = nbuf[...].reshape(128, 1024)
    tn = ((0,), (0,))
    hbuf[:, :, 0:32, :] = dot(normed, rg_top, tn).reshape(4, 8, 32, 128).astype(BF16)
    hbuf[:, :, 32:64, :] = dot(normed, rg_bottom, tn).reshape(4, 8, 32, 128).astype(BF16)
    h1a = over_y(lambda t: hbuf.at[:, t, wa], lambda d: ha1.at[d - 1])
    h1b = over_x(lambda t: hbuf.at[t, :, wb], lambda d: hb1.at[d - 1])
    arrived(h1a)
    hta[...] = (hbuf[:, y, 0:16].astype(F32) + jnp.sum(ha1[...].astype(F32), axis=0)).astype(BF16)
    h2a = over_x(lambda t: hta.at[t], lambda d: ha2.at[d - 1])
    arrived(h1b)
    htb[...] = (hbuf[x, :, 16:64].astype(F32) + jnp.sum(hb1[...].astype(F32), axis=0)).astype(BF16)
    h2b = over_y(lambda t: htb.at[t], lambda d: hb2.at[d - 1])
    arrived(h2a)
    h_a = hta[x].astype(F32) + jnp.sum(ha2[...].astype(F32), axis=0)
    arrived(h2b)
    h_b = htb[y].astype(F32) + jnp.sum(hb2[...].astype(F32), axis=0)
    hz[0, 0:16] = h_a
    hz[0, 16:32] = h_b[0:16]
    hz[1] = h_b[16:48]
    c_h = cp(hz.at[1 - zlo], hzr, dev(z=z + 1 - 2 * zlo))

    arrived(c_s)
    su_f = s_f * s_scale
    g0 = spbuf[z, 0].astype(F32)
    g1 = spbuf[z, 1].astype(F32)
    for d in range(7):
        g0 += srecv[d, 0].astype(F32)
        g1 += srecv[d, 1].astype(F32)
    usg = jnp.concatenate([g0, g1], axis=1)
    inner_s = jnp.sum(su_f * usg, axis=1, keepdims=True)
    sg_out[...] = (s_scale * (usg - su_f * inner_s)).astype(BF16)

    c_h.wait_recv()
    hg_out[...] = hz[zlo] + hzr[...]
    for copy in started:
        copy.wait_send()


def body(features, gain, weights, states, ids, sharpness, offset):
    core = lax.rem(lax.axis_index("param"), 2)
    z = (lax.axis_index("param") // 2) * 2 + lax.axis_index("batch") // 32
    lane = lax.broadcasted_iota(jnp.int32, (8, 128), 1)
    twice = jnp.concatenate([ids, ids])[None, :]
    idrow = jnp.where(lane // 64 == lax.rem(z, 2), twice, 0)
    vmem = pl.BlockSpec(memory_space=pltpu.VMEM)
    smem = pl.BlockSpec(memory_space=pltpu.SMEM)
    V = pltpu.VMEM
    return pl.pallas_call(
        kernel,
        out_shape=(
            jax.ShapeDtypeStruct((64, 1024), BF16),
            jax.ShapeDtypeStruct((32, 128), F32),
        ),
        in_specs=[vmem] * 5 + [smem] * 2,
        out_specs=(vmem, vmem),
        scratch_shapes=[
            V((4, 2, 16, 1024), BF16),
            V((4, 8, 64, 128), BF16),
            V((4, 16, 128), BF16),
            V((8, 16, 128), BF16),
            V((2, 16, 512), BF16),
            V((2, 4, 8, 16, 512), BF16),
            V((2, 8, 64, 512), BF16),
            V((8, 8, 128), jnp.int32),
            V((512, 512), BF16),
            V((4, 8, 16, 512), F32),
            V((4, 8, 16, 512), BF16),
            V((4, 8, 16, 512), BF16),
            V((4, 8, 16, 512), BF16),
            V((7, 4, 16, 128), BF16),
            V((3, 8, 16, 384), BF16),
            V((4, 16, 128), BF16),
            V((8, 16, 384), BF16),
            V((3, 16, 128), BF16),
            V((7, 16, 384), BF16),
            V((2, 16, 512), F32),
            V((8, 16, 128), BF16),
            V((4, 16, 128), BF16),
            V((4, 8, 64, 128), BF16),
            V((7, 4, 16, 128), BF16),
            V((3, 8, 48, 128), BF16),
            V((4, 16, 128), BF16),
            V((8, 48, 128), BF16),
            V((3, 16, 128), BF16),
            V((7, 48, 128), BF16),
            V((2, 32, 128), F32),
            V((32, 128), F32),
            V((8, 2, 64, 512), BF16),
            V((7, 2, 64, 512), BF16),
            pltpu.SemaphoreType.DMA((N_SEM,)),
            pltpu.SemaphoreType.DMA((N_SEM,)),
        ],
        compiler_params=pltpu.CompilerParams(
            collective_id=0, has_side_effects=True, vmem_limit_bytes=48 * 2**20
        ),
    )(features, gain.reshape(1, 2048), weights, states, idrow, sharpness, offset)


def solution(mesh):
    in_specs = (
        P(("batch", "param"), None),
        P(),
        P("batch", "param"),
        P(("batch", "param"), None),
        P(("batch", "param")),
        P(),
        P(),
    )
    out_specs = (P(("batch", "param"), None), P("batch", "param"))
    return jax.shard_map(body, mesh=mesh, in_specs=in_specs, out_specs=out_specs, check_vma=False)
```

```python
import jax
import jax.numpy as jnp
from jax import lax
from jax.experimental import pallas as pl
from jax.experimental.pallas import tpu as pltpu
from jax.sharding import PartitionSpec as P

F32 = jnp.float32
BF16 = jnp.bfloat16
MESH = pl.DeviceIdType.MESH
NX, NY, NZ = 4, 8, 8
N_SEM = 160
FAR_Y = (4, 3, 5, 2, 6, 1, 7)
FAR_X = (2, 1, 3)


def dot(a, b, contract=((1,), (0,))):
    return lax.dot_general(a, b, (contract, ((), ())), preferred_element_type=F32)


def kernel(
    feat_in, gain_in, wblk_in, src_in, idrow_in, sharp, shift,
    sg_out, hg_out,
    feat, gain, wblk, src, idrow, nbuf, wbuf, rpart, rbuf, gown, gbuf, sbuf, idbuf, pt,
    uown, usend, urecv, ub, ua1, ub1, ta, tb, ua2, ub2, xbuf,
    rgb, rgr, hbuf, ha1, hb1, hta, htb, ha2, hb2, hz, hzr,
    spbuf, srecv, send_sem, recv_sem, in_sem,
):
    b = lax.axis_index("batch")
    p = lax.axis_index("param")
    zlo = b // 32
    x = lax.rem(b // 8, NX)
    y = lax.rem(b, NY)
    zhi = p // 2
    core = lax.rem(p, 2)
    z = zhi * 2 + zlo

    def dev(x=x, y=y, z=z, core=core):
        return (lax.rem(z, 2) * 32 + x * 8 + y, (z // 2) * 2 + core)

    def xd(d):
        return lax.rem(x + d, NX)

    def yd(d):
        return lax.rem(y + d, NY)

    def zd(d):
        return lax.rem(z + d, NZ)

    loads = [
        pltpu.make_async_copy(a, c, in_sem.at[i])
        for i, (a, c) in enumerate(
            ((wblk_in, wblk), (feat_in, feat), (gain_in, gain), (src_in, src), (idrow_in, idrow))
        )
    ]
    for load in loads:
        load.start()

    peers = [dev(y=yd(d)) for d in range(1, NY)]
    peers += [dev(x=xd(d)) for d in range(1, NX)]
    peers += [dev(z=zd(d)) for d in range(1, NZ)]
    peers += [dev(z=zd(d), core=1 - core) for d in (0, 2, 4, 6)]
    barrier = pltpu.get_barrier_semaphore()
    for peer in peers:
        pl.semaphore_signal(barrier, inc=1, device_id=peer, device_id_type=MESH)

    for load in loads:
        load.wait()
    f = feat[...].astype(F32)
    nf = f * lax.rsqrt(jnp.mean(f * f, axis=1, keepdims=True) + 1e-6) * gain[...]
    nbuf[zhi, core] = jnp.concatenate([nf[:, :1024], nf[:, 1024:]], axis=0).astype(BF16)
    wbuf[x, y, pl.ds(pl.multiple_of(zlo * 32, 32), 32), :] = wblk[...]
    idbuf[z] = idrow[...]
    s_f = src[...].astype(F32)
    s_scale = lax.rsqrt(jnp.sum(s_f * s_f, axis=1, keepdims=True) + 1e-6)
    s_unit = (s_f * s_scale).astype(BF16)
    sbuf[0, z] = s_unit[:, :512]
    sbuf[1, z] = s_unit[:, 512:]

    pl.semaphore_wait(barrier, len(peers))

    started = []

    def cp(a, c, device):
        i = len(started)
        copy = pltpu.make_async_remote_copy(
            src_ref=a, dst_ref=c, send_sem=send_sem.at[i], recv_sem=recv_sem.at[i],
            device_id=device, device_id_type=MESH,
        )
        copy.start()
        started.append(copy)
        return copy

    def arrived(copies):
        for copy in copies:
            copy.wait_recv()

    def over_x(src_of, dst_of):
        return [cp(src_of(xd(d)), dst_of(d), dev(x=xd(d))) for d in FAR_X]

    def over_y(src_of, dst_of):
        return [cp(src_of(yd(d)), dst_of(d), dev(y=yd(d))) for d in FAR_Y]

    wz = wbuf.at[x, y, pl.ds(pl.multiple_of(zlo * 32, 32), 32), :]
    c_wz = cp(wz, wz, dev(z=z + 1 - 2 * zlo))
    c_n = [cp(nbuf.at[zhi, core], nbuf.at[zhi, core], dev(z=zd(d))) for d in (4, 2, 6)]
    c_wz.wait_recv()
    wa, wb = pl.ds(0, 16), pl.ds(16, 48)
    w1a = over_x(lambda t: wbuf.at[x, y, wa], lambda d: wbuf.at[x, y, wa])
    w1b = over_y(lambda t: wbuf.at[x, y, wb], lambda d: wbuf.at[x, y, wb])

    def hop(block, rows, step):
        ref = sbuf.at[:, block, rows]
        return cp(ref, ref, dev(z=zd(step)))

    every, low, high = pl.ds(0, 64), pl.ds(0, 32), pl.ds(32, 32)
    s_up, s_down = hop(z, every, 1), hop(z, every, 7)
    c_id = [cp(idbuf.at[z], idbuf.at[z], dev(z=zd(d))) for d in range(1, NZ)]

    arrived(w1a)
    w2a = over_y(lambda t: wbuf.at[:, y, wa], lambda d: wbuf.at[:, y, wa])
    arrived(w1b)
    w2b = over_x(lambda t: wbuf.at[x, :, wb], lambda d: wbuf.at[x, :, wb])
    arrived(c_n)
    c_ns = cp(nbuf.at[:, core], nbuf.at[:, core], dev(core=1 - core))
    s_up.wait_recv()
    s_down.wait_recv()
    s_up, s_down = hop(zd(7), every, 1), hop(zd(1), every, 7)
    c_ns.wait_recv()
    arrived(w2a)
    arrived(w2b)

    normed = nbuf[...].reshape(128, 1024)
    top = dot(normed, wbuf[:, :, 0:32, :].reshape(1024, 128)).reshape(8, 16, 128)
    bottom = dot(normed, wbuf[:, :, 32:64, :].reshape(1024, 128)).reshape(8, 16, 128)
    rpart[...] = (top[:, 0:8] + bottom[:, 8:16]).reshape(4, 16, 128).astype(BF16)
    rbuf[p] = rpart[zhi]
    c_r = []
    for d in (4, 2, 6, 0):
        to = zd(d)
        if d:
            c_r.append(cp(rpart.at[to // 2], rbuf.at[p], dev(z=to)))
        c_r.append(cp(rpart.at[to // 2], rbuf.at[p], dev(z=to, core=1 - core)))
    arrived(c_r)

    raw_f = jnp.concatenate([rbuf[k] for k in range(8)], axis=1).astype(F32)
    g_scale = lax.rsqrt(jnp.sum(raw_f * raw_f, axis=1, keepdims=True) + 1e-6)
    g_unit = (raw_f * g_scale).astype(BF16)
    gown[0] = g_unit[:, :512]
    gown[1] = g_unit[:, 512:]
    gbuf[core, x, y] = gown[core]
    ga, gb = pl.ds(0, 128), pl.ds(128, 384)
    g1a = over_x(lambda t: gbuf.at[core, x, y, :, ga], lambda d: gbuf.at[core, x, y, :, ga])
    g1b = over_y(lambda t: gbuf.at[core, x, y, :, gb], lambda d: gbuf.at[core, x, y, :, gb])
    s_up.wait_recv()
    s_down.wait_recv()
    s_up, s_down = hop(zd(6), every, 1), hop(zd(2), every, 7)
    arrived(g1a)
    g2a = over_y(lambda t: gbuf.at[core, :, y, :, ga], lambda d: gbuf.at[core, :, y, :, ga])
    arrived(g1b)
    mine = gbuf.at[core, x, :, :, gb]
    g2b = {d: cp(mine, mine, dev(x=xd(d))) for d in FAR_X}
    s_up.wait_recv()
    s_down.wait_recv()
    s_up, s_down = hop(zd(5), low, 1), hop(zd(3), high, 7)
    arrived(g2a)

    sibling = dev(core=1 - core)
    c_g, c_u, u1b = {}, {}, []

    def share(d):
        if d:
            g2b[NX - d].wait_recv()
        block = gbuf.at[core, xd(d)]
        c_g[d] = cp(block, block, sibling)

    def weigh(d):
        k = xd(d)
        c_g[d].wait_recv()
        nt = ((1,), (1,))
        sim = dot(gbuf[0, k].reshape(128, 512), sbuf[0].reshape(512, 512), nt)
        sim += dot(gbuf[1, k].reshape(128, 512), sbuf[1].reshape(512, 512), nt)
        logits = scale * sim + offset
        goal = (zlo * 32 + k * 8 + row // 16) * 64 + zhi * 16 + lax.rem(row, 16)
        sign = jnp.where(goal == ids, 1.0, -1.0).astype(F32)
        weight = (-scale * sign / (1.0 + jnp.exp(sign * logits))).astype(BF16)
        pt[pl.ds(pl.multiple_of(k * 128, 128), 128), :] = weight
        usend[k] = dot(weight, sbuf[1 - core].reshape(512, 512)).reshape(8, 16, 512).astype(BF16)
        c_u[d] = cp(usend.at[k], urecv.at[k], sibling)
        uown[k] = dot(weight, sbuf[core].reshape(512, 512)).reshape(8, 16, 512)

    def pass_on(d):
        k = xd(d)
        c_u[d].wait_recv()
        ub[k] = (uown[k] + urecv[k].astype(F32)).astype(BF16)
        if d:
            u1b.append(cp(ub.at[k, :, :, gb], ub1.at[d - 1], dev(x=k)))

    share(0)
    scale, offset = sharp[0], shift[0]
    row = lax.broadcasted_iota(jnp.int32, (128, 1), 0)
    arrived(c_id)
    ids = jnp.concatenate(
        [idbuf[2 * q, 0:1] + idbuf[2 * q + 1, 0:1] for q in range(4)], axis=1
    )
    s_up.wait_recv()
    s_down.wait_recv()
    share(1)
    weigh(0)
    share(3)
    weigh(1)
    pass_on(0)
    share(2)
    weigh(3)
    pass_on(1)
    weigh(2)
    pass_on(3)
    pass_on(2)
    u1a = over_y(lambda t: ub.at[:, t, :, ga], lambda d: ua1.at[d - 1])

    for q in range(4):
        lhs = pt[:, q * 128:(q + 1) * 128]
        for h in range(2):
            part = dot(lhs, gbuf[h].reshape(512, 512), ((0,), (0,)))
            spbuf[2 * q:2 * q + 2, h] = part.reshape(2, 64, 512).astype(BF16)

    def scatter_states(ds):
        return [cp(spbuf.at[zd(d)], srecv.at[d - 1], dev(z=zd(d))) for d in ds]

    c_s = scatter_states((3, 5, 1, 7))
    arrived(u1a)
    ta[...] = (ub[:, y, :, 0:128].astype(F32) + jnp.sum(ua1[...].astype(F32), axis=0)).astype(BF16)
    u2a = over_x(lambda t: ta.at[t], lambda d: ua2.at[d - 1])
    arrived(u1b)
    tb[...] = (ub[x, :, :, 128:512].astype(F32) + jnp.sum(ub1[...].astype(F32), axis=0)).astype(BF16)
    u2b = over_y(lambda t: tb.at[t], lambda d: ub2.at[d - 1])
    arrived(u2a)
    xbuf[core, :, 0:128] = ta[x].astype(F32) + jnp.sum(ua2[...].astype(F32), axis=0)
    arrived(u2b)
    xbuf[core, :, 128:512] = tb[y].astype(F32) + jnp.sum(ub2[...].astype(F32), axis=0)
    c_x = cp(xbuf.at[core], xbuf.at[core], dev(core=1 - core))
    c_x.wait_recv()

    u = jnp.concatenate([xbuf[0], xbuf[1]], axis=1)
    g_f = raw_f * g_scale
    inner = jnp.sum(g_f * u, axis=1, keepdims=True)
    raw_grad = (g_scale * (u - g_f * inner)).astype(BF16)
    for k in range(8):
        rgb[k] = raw_grad[:, k * 128:(k + 1) * 128]
    rgr[zhi] = rgb[p]
    c_rg = [cp(rgb.at[(zd(d) // 2) * 2 + core], rgr.at[zhi], dev(z=zd(d))) for d in (4, 2, 6)]
    c_s += scatter_states((4, 2, 6))
    arrived(c_rg)
    rg = rgr[...].astype(F32).reshape(8, 8, 128)
    zero = jnp.zeros((8, 8, 128), F32)
    rg_top = jnp.concatenate([rg, zero], axis=1).reshape(128, 128).astype(BF16)
    rg_bottom = jnp.concatenate([zero, rg], axis=1).reshape(128, 128).astype(BF16)
    normed = nbuf[...].reshape(128, 1024)
    tn = ((0,), (0,))
    hbuf[:, :, 0:32, :] = dot(normed, rg_top, tn).reshape(4, 8, 32, 128).astype(BF16)
    hbuf[:, :, 32:64, :] = dot(normed, rg_bottom, tn).reshape(4, 8, 32, 128).astype(BF16)
    h1a = over_y(lambda t: hbuf.at[:, t, wa], lambda d: ha1.at[d - 1])
    h1b = over_x(lambda t: hbuf.at[t, :, wb], lambda d: hb1.at[d - 1])
    arrived(h1a)
    hta[...] = (hbuf[:, y, 0:16].astype(F32) + jnp.sum(ha1[...].astype(F32), axis=0)).astype(BF16)
    h2a = over_x(lambda t: hta.at[t], lambda d: ha2.at[d - 1])
    arrived(h1b)
    htb[...] = (hbuf[x, :, 16:64].astype(F32) + jnp.sum(hb1[...].astype(F32), axis=0)).astype(BF16)
    h2b = over_y(lambda t: htb.at[t], lambda d: hb2.at[d - 1])
    arrived(h2a)
    h_a = hta[x].astype(F32) + jnp.sum(ha2[...].astype(F32), axis=0)
    arrived(h2b)
    h_b = htb[y].astype(F32) + jnp.sum(hb2[...].astype(F32), axis=0)
    hz[0, 0:16] = h_a
    hz[0, 16:32] = h_b[0:16]
    hz[1] = h_b[16:48]
    c_h = cp(hz.at[1 - zlo], hzr, dev(z=z + 1 - 2 * zlo))

    arrived(c_s)
    su_f = s_f * s_scale
    g0 = spbuf[z, 0].astype(F32)
    g1 = spbuf[z, 1].astype(F32)
    for d in range(7):
        g0 += srecv[d, 0].astype(F32)
        g1 += srecv[d, 1].astype(F32)
    usg = jnp.concatenate([g0, g1], axis=1)
    inner_s = jnp.sum(su_f * usg, axis=1, keepdims=True)
    sg_out[...] = (s_scale * (usg - su_f * inner_s)).astype(BF16)

    c_h.wait_recv()
    hg_out[...] = hz[zlo] + hzr[...]
    for copy in started:
        copy.wait_send()


def body(features, gain, weights, states, ids, sharpness, offset):
    core = lax.rem(lax.axis_index("param"), 2)
    z = (lax.axis_index("param") // 2) * 2 + lax.axis_index("batch") // 32
    lane = lax.broadcasted_iota(jnp.int32, (8, 128), 1)
    twice = jnp.concatenate([ids, ids])[None, :]
    idrow = jnp.where(lane // 64 == lax.rem(z, 2), twice, 0)
    vmem = pl.BlockSpec(memory_space=pltpu.VMEM)
    hbm = pl.BlockSpec(memory_space=pltpu.HBM)
    smem = pl.BlockSpec(memory_space=pltpu.SMEM)
    V = pltpu.VMEM
    return pl.pallas_call(
        kernel,
        out_shape=(
            jax.ShapeDtypeStruct((64, 1024), BF16),
            jax.ShapeDtypeStruct((32, 128), F32),
        ),
        in_specs=[hbm] * 5 + [smem] * 2,
        out_specs=(vmem, vmem),
        scratch_shapes=[
            V((8, 2048), BF16),
            V((1, 2048), F32),
            V((32, 128), BF16),
            V((64, 1024), BF16),
            V((8, 128), jnp.int32),
            V((4, 2, 16, 1024), BF16),
            V((4, 8, 64, 128), BF16),
            V((4, 16, 128), BF16),
            V((8, 16, 128), BF16),
            V((2, 16, 512), BF16),
            V((2, 4, 8, 16, 512), BF16),
            V((2, 8, 64, 512), BF16),
            V((8, 8, 128), jnp.int32),
            V((512, 512), BF16),
            V((4, 8, 16, 512), F32),
            V((4, 8, 16, 512), BF16),
            V((4, 8, 16, 512), BF16),
            V((4, 8, 16, 512), BF16),
            V((7, 4, 16, 128), BF16),
            V((3, 8, 16, 384), BF16),
            V((4, 16, 128), BF16),
            V((8, 16, 384), BF16),
            V((3, 16, 128), BF16),
            V((7, 16, 384), BF16),
            V((2, 16, 512), F32),
            V((8, 16, 128), BF16),
            V((4, 16, 128), BF16),
            V((4, 8, 64, 128), BF16),
            V((7, 4, 16, 128), BF16),
            V((3, 8, 48, 128), BF16),
            V((4, 16, 128), BF16),
            V((8, 48, 128), BF16),
            V((3, 16, 128), BF16),
            V((7, 48, 128), BF16),
            V((2, 32, 128), F32),
            V((32, 128), F32),
            V((8, 2, 64, 512), BF16),
            V((7, 2, 64, 512), BF16),
            pltpu.SemaphoreType.DMA((N_SEM,)),
            pltpu.SemaphoreType.DMA((N_SEM,)),
            pltpu.SemaphoreType.DMA((5,)),
        ],
        compiler_params=pltpu.CompilerParams(
            collective_id=0, has_side_effects=True, vmem_limit_bytes=48 * 2**20
        ),
    )(features, gain.reshape(1, 2048), weights, states, idrow, sharpness, offset)


def solution(mesh):
    in_specs = (
        P(("batch", "param"), None),
        P(),
        P("batch", "param"),
        P(("batch", "param"), None),
        P(("batch", "param")),
        P(),
        P(),
    )
    out_specs = (P(("batch", "param"), None), P("batch", "param"))
    return jax.shard_map(body, mesh=mesh, in_specs=in_specs, out_specs=out_specs, check_vma=False)
```

```python
import jax
import jax.numpy as jnp
from jax import lax
from jax.experimental import pallas as pl
from jax.experimental.pallas import tpu as pltpu
from jax.sharding import PartitionSpec as P

F32 = jnp.float32
BF16 = jnp.bfloat16
MESH = pl.DeviceIdType.MESH
NX, NY, NZ = 4, 8, 8
N_SEM = 208
FAR_Y = (4, 3, 5, 2, 6, 1, 7)
FAR_X = (2, 1, 3)


def dot(a, b, contract=((1,), (0,))):
    return lax.dot_general(a, b, (contract, ((), ())), preferred_element_type=F32)


def kernel(
    feat_in, gain_in, wblk_in, src_in, idrow_in, sharp, shift,
    sg_out, hg_out,
    feat, gain, wblk, src, idrow, nsend, nq, wq, rpart, rbuf, gown, gbuf, sbuf, idbuf, pt,
    uown, usend, urecv, ub, ua1, ub1, ta, tb, ua2, ub2, xbuf,
    rgb, rgr, nt_buf, hq, hsum,
    spbuf, shalf, srecv, send_sem, recv_sem, in_sem,
):
    b = lax.axis_index("batch")
    p = lax.axis_index("param")
    zlo = b // 32
    x = lax.rem(b // 8, NX)
    y = lax.rem(b, NY)
    zhi = p // 2
    core = lax.rem(p, 2)
    z = zhi * 2 + zlo
    zp = z + 1 - 2 * zlo

    def dev(x=x, y=y, z=z, core=core):
        return (lax.rem(z, 2) * 32 + x * 8 + y, (z // 2) * 2 + core)

    def xd(d):
        return lax.rem(x + d, NX)

    def yd(d):
        return lax.rem(y + d, NY)

    def zd(d):
        return lax.rem(z + d, NZ)

    loads = [
        pltpu.make_async_copy(a, c, in_sem.at[i])
        for i, (a, c) in enumerate(
            ((wblk_in, wblk), (feat_in, feat), (gain_in, gain), (src_in, src), (idrow_in, idrow))
        )
    ]
    for load in loads:
        load.start()

    peers = [dev(y=yd(d)) for d in range(1, NY)]
    peers += [dev(y=yd(d), z=zp) for d in range(1, NY)]
    peers += [dev(z=zd(d)) for d in range(1, NZ)]
    peers += [dev(x=xd(d), z=zd(e)) for d in (1, 2, 3) for e in (0, 2, 4, 6)]
    peers += [dev(x=xd(d), z=zd(e), core=1 - core) for d in (0, 1, 2, 3) for e in (0, 2, 4, 6)]
    barrier = pltpu.get_barrier_semaphore()
    for peer in peers:
        pl.semaphore_signal(barrier, inc=1, device_id=peer, device_id_type=MESH)

    for load in loads:
        load.wait()
    f = feat[...].astype(F32)
    nf = f * lax.rsqrt(jnp.mean(f * f, axis=1, keepdims=True) + 1e-6) * gain[...]
    n16 = jnp.concatenate([nf[:, :1024], nf[:, 1024:]], axis=0).astype(BF16)
    for k in range(NX):
        nsend[k] = n16[:, k * 256:(k + 1) * 256]
    nq[x, zhi, core] = nsend[x]
    wq[zlo, y] = wblk[...]
    lane = lax.broadcasted_iota(jnp.int32, (8, 128), 1)
    twice = jnp.broadcast_to(jnp.concatenate([idrow[...], idrow[...]], axis=1), (8, 128))
    idbuf[z] = jnp.where(lane // 64 == zlo, twice, 0)
    s_f = src[...].astype(F32)
    s_scale = lax.rsqrt(jnp.sum(s_f * s_f, axis=1, keepdims=True) + 1e-6)
    s_unit = (s_f * s_scale).astype(BF16)
    sbuf[0, z] = s_unit[:, :512]
    sbuf[1, z] = s_unit[:, 512:]

    pl.semaphore_wait(barrier, len(peers))

    started = []

    def cp(a, c, device):
        i = len(started)
        copy = pltpu.make_async_remote_copy(
            src_ref=a, dst_ref=c, send_sem=send_sem.at[i], recv_sem=recv_sem.at[i],
            device_id=device, device_id_type=MESH,
        )
        copy.start()
        started.append(copy)
        return copy

    def arrived(copies):
        for copy in copies:
            copy.wait_recv()

    def over_x(src_of, dst_of):
        return [cp(src_of(xd(d)), dst_of(d), dev(x=xd(d))) for d in FAR_X]

    def over_y(src_of, dst_of):
        return [cp(src_of(yd(d)), dst_of(d), dev(y=yd(d))) for d in FAR_Y]

    def over_zy(src_of, dst_of):
        return [
            cp(src_of(f, yd(d)), dst_of(NY * f + d), dev(y=yd(d), z=zp if f else z))
            for d in FAR_Y + (0,) for f in (1, 0) if f or d
        ]

    XZ = [(d, e) for e in (4, 2, 6, 0) for d in FAR_X + (0,)]
    own_w = wq.at[zlo, y]
    w1 = over_zy(lambda f, t: own_w, lambda i: own_w)
    c_n = [
        cp(nsend.at[xd(d)], nq.at[x, zhi, core], dev(x=xd(d), z=zd(e)))
        for d, e in XZ if d or e
    ]

    def hop(block, rows, step):
        ref = sbuf.at[:, block, rows]
        return cp(ref, ref, dev(z=zd(step)))

    every, low, high = pl.ds(0, 64), pl.ds(0, 32), pl.ds(32, 32)
    s_up, s_down = hop(z, every, 1), hop(z, every, 7)
    c_id = [cp(idbuf.at[z], idbuf.at[z], dev(z=zd(d))) for d in range(1, NZ)]

    arrived(c_n)
    c_ns = cp(nq.at[:, :, core], nq.at[:, :, core], dev(core=1 - core))
    arrived(w1)
    c_ns.wait_recv()

    halves = jnp.concatenate([wq[0].reshape(256, 128), wq[1].reshape(256, 128)], axis=1)
    both = dot(nq[...].reshape(512, 256), halves).reshape(32, 16, 256)
    rpart[...] = (both[:, 0:8, :128] + both[:, 8:16, 128:]).reshape(4, 4, 16, 128).astype(BF16)
    c_r = [
        cp(
            rpart.at[xd(d), zd(e) // 2], rbuf.at[x, p],
            dev(x=xd(d), z=zd(e), core=1 - core if flip else core),
        )
        for d, e in XZ for flip in (1, 0) if d or e or flip
    ]
    rbuf[x, p] = rpart[x, zhi]
    s_up.wait_recv()
    s_down.wait_recv()
    s_up, s_down = hop(zd(7), every, 1), hop(zd(1), every, 7)
    nt_buf[...] = nq[...].reshape(512, 256).T
    arrived(c_r)

    raw = jnp.sum(rbuf[...].astype(F32), axis=0).astype(BF16)
    raw_f = jnp.concatenate([raw[k] for k in range(8)], axis=1).astype(F32)
    g_scale = lax.rsqrt(jnp.sum(raw_f * raw_f, axis=1, keepdims=True) + 1e-6)
    g_unit = (raw_f * g_scale).astype(BF16)
    gown[0] = g_unit[:, :512]
    gown[1] = g_unit[:, 512:]
    gbuf[core, x, y] = gown[core]
    ga, gb = pl.ds(0, 128), pl.ds(128, 384)
    g1a = over_x(lambda t: gbuf.at[core, x, y, :, ga], lambda d: gbuf.at[core, x, y, :, ga])
    g1b = over_y(lambda t: gbuf.at[core, x, y, :, gb], lambda d: gbuf.at[core, x, y, :, gb])
    s_up.wait_recv()
    s_down.wait_recv()
    s_up, s_down = hop(zd(6), every, 1), hop(zd(2), every, 7)
    arrived(g1a)
    g2a = over_y(lambda t: gbuf.at[core, :, y, :, ga], lambda d: gbuf.at[core, :, y, :, ga])
    arrived(g1b)
    mine = gbuf.at[core, x, :, :, gb]
    g2b = {d: cp(mine, mine, dev(x=xd(d))) for d in FAR_X}
    s_up.wait_recv()
    s_down.wait_recv()
    s_up, s_down = hop(zd(5), low, 1), hop(zd(3), high, 7)
    arrived(g2a)

    sibling = dev(core=1 - core)
    c_g, c_u, u1b = {}, {}, []

    def share(d):
        if d:
            g2b[NX - d].wait_recv()
        block = gbuf.at[core, xd(d)]
        c_g[d] = cp(block, block, sibling)

    def weigh(pair):
        nt = ((1,), (1,))
        ks = [xd(d) for d in pair]
        for d in pair:
            c_g[d].wait_recv()
        g0, g1 = (
            jnp.concatenate([gbuf[h, k].reshape(128, 512) for k in ks], axis=0) for h in (0, 1)
        )
        sim = dot(g0, sbuf[0].reshape(512, 512), nt) + dot(g1, sbuf[1].reshape(512, 512), nt)
        logits = scale * sim + offset
        goal = jnp.concatenate(
            [(zlo * 32 + k * 8 + row // 16) * 64 + zhi * 16 + lax.rem(row, 16) for k in ks], axis=0
        )
        sign = jnp.where(goal == ids, 1.0, -1.0).astype(F32)
        weight = (-scale * sign / (1.0 + jnp.exp(sign * logits))).astype(BF16)
        for i, k in enumerate(ks):
            pt[pl.ds(pl.multiple_of(k * 128, 128), 128), :] = weight[i * 128:(i + 1) * 128]
        give = dot(weight, sbuf[1 - core].reshape(512, 512)).astype(BF16)
        for i, (d, k) in enumerate(zip(pair, ks)):
            usend[k] = give[i * 128:(i + 1) * 128].reshape(8, 16, 512)
            c_u[d] = cp(usend.at[k], urecv.at[k], sibling)
        keep = dot(weight, sbuf[core].reshape(512, 512))
        for i, k in enumerate(ks):
            uown[k] = keep[i * 128:(i + 1) * 128].reshape(8, 16, 512)

    def pass_on(d):
        k = xd(d)
        c_u[d].wait_recv()
        ub[k] = (uown[k] + urecv[k].astype(F32)).astype(BF16)
        if d:
            u1b.append(cp(ub.at[k, :, :, gb], ub1.at[d - 1], dev(x=k)))

    share(0)
    scale, offset = sharp[0], shift[0]
    row = lax.broadcasted_iota(jnp.int32, (128, 1), 0)
    arrived(c_id)
    ids = jnp.concatenate(
        [idbuf[2 * q, 0:1] + idbuf[2 * q + 1, 0:1] for q in range(4)], axis=1
    )
    s_up.wait_recv()
    s_down.wait_recv()
    share(1)
    weigh((0, 1))
    share(3)
    share(2)
    pass_on(1)
    pass_on(0)
    weigh((3, 2))
    pass_on(2)
    pass_on(3)
    u1a = over_y(lambda t: ub.at[:, t, :, ga], lambda d: ua1.at[d - 1])

    for q in range(4):
        lhs = pt[:, q * 128:(q + 1) * 128]
        for h in range(2):
            part = dot(lhs, gbuf[h].reshape(512, 512), ((0,), (0,)))
            spbuf[2 * q:2 * q + 2, h] = part.reshape(2, 64, 512).astype(BF16)

    low32, high32 = pl.ds(0, 32), pl.ds(32, 32)
    r_up = cp(spbuf.at[zd(4), :, low32], shalf.at[0], dev(z=zd(1)))
    r_down = cp(spbuf.at[zd(4), :, high32], shalf.at[1], dev(z=zd(7)))

    def relay(step, r_up, r_down):
        r_up.wait_recv()
        r_down.wait_recv()
        up, down = zd(4 - step), zd(4 + step)
        if step == 1:
            spbuf[up, :, 0:32] = (spbuf[up, :, 0:32].astype(F32) + shalf[0].astype(F32)).astype(BF16)
            spbuf[down, :, 32:64] = (spbuf[down, :, 32:64].astype(F32) + shalf[1].astype(F32)).astype(BF16)
        else:
            spbuf[up] = (spbuf[up].astype(F32) + srecv[step - 2, 0].astype(F32)).astype(BF16)
            spbuf[down] = (spbuf[down].astype(F32) + srecv[step - 2, 1].astype(F32)).astype(BF16)
        return (
            cp(spbuf.at[up], srecv.at[step - 1, 0], dev(z=zd(1))),
            cp(spbuf.at[down], srecv.at[step - 1, 1], dev(z=zd(7))),
        )

    arrived(u1a)
    ta[...] = (ub[:, y, :, 0:128].astype(F32) + jnp.sum(ua1[...].astype(F32), axis=0)).astype(BF16)
    u2a = over_x(lambda t: ta.at[t], lambda d: ua2.at[d - 1])
    arrived(u1b)
    tb[...] = (ub[x, :, :, 128:512].astype(F32) + jnp.sum(ub1[...].astype(F32), axis=0)).astype(BF16)
    u2b = over_y(lambda t: tb.at[t], lambda d: ub2.at[d - 1])
    r_up, r_down = relay(1, r_up, r_down)
    arrived(u2a)
    xbuf[core, :, 0:128] = ta[x].astype(F32) + jnp.sum(ua2[...].astype(F32), axis=0)
    arrived(u2b)
    xbuf[core, :, 128:512] = tb[y].astype(F32) + jnp.sum(ub2[...].astype(F32), axis=0)
    c_x = cp(xbuf.at[core], xbuf.at[core], dev(core=1 - core))
    r_up, r_down = relay(2, r_up, r_down)
    c_x.wait_recv()

    u = jnp.concatenate([xbuf[0], xbuf[1]], axis=1)
    g_f = raw_f * g_scale
    inner = jnp.sum(g_f * u, axis=1, keepdims=True)
    raw_grad = (g_scale * (u - g_f * inner)).astype(BF16)
    for k in range(8):
        rgb[k] = raw_grad[:, k * 128:(k + 1) * 128]
    rgr[x, zhi] = rgb[p]
    c_rg = [
        cp(rgb.at[(zd(e) // 2) * 2 + core], rgr.at[x, zhi], dev(x=xd(d), z=zd(e)))
        for d, e in XZ if d or e
    ]
    r_up, r_down = relay(3, r_up, r_down)
    arrived(c_rg)
    rg = rgr[...].astype(F32).reshape(32, 8, 128)
    zero = jnp.zeros((32, 8, 128), F32)
    rg_top = jnp.concatenate([rg, zero], axis=1).reshape(512, 128).astype(BF16)
    rg_bottom = jnp.concatenate([zero, rg], axis=1).reshape(512, 128).astype(BF16)
    part = dot(nt_buf[...], jnp.concatenate([rg_top, rg_bottom], axis=1)).astype(BF16)
    hq[0] = part[:, :128].reshape(8, 32, 128)
    hq[1] = part[:, 128:].reshape(8, 32, 128)
    c_h = over_zy(lambda f, t: hq.at[1 - zlo if f else zlo, t], lambda i: hsum.at[i])
    hsum[0] = hq[zlo, y]

    r_up.wait_recv()
    r_down.wait_recv()
    su_f = s_f * s_scale
    sums = spbuf[z].astype(F32) + srecv[2, 0].astype(F32) + srecv[2, 1].astype(F32)
    usg = jnp.concatenate([sums[0], sums[1]], axis=1)
    inner_s = jnp.sum(su_f * usg, axis=1, keepdims=True)
    sg_out[...] = (s_scale * (usg - su_f * inner_s)).astype(BF16)

    arrived(c_h)
    hg_out[...] = jnp.sum(hsum[...].astype(F32), axis=0)
    for copy in started:
        copy.wait_send()


def body(features, gain, weights, states, ids, sharpness, offset):
    vmem = pl.BlockSpec(memory_space=pltpu.VMEM)
    hbm = pl.BlockSpec(memory_space=pltpu.HBM)
    smem = pl.BlockSpec(memory_space=pltpu.SMEM)
    V = pltpu.VMEM
    return pl.pallas_call(
        kernel,
        out_shape=(
            jax.ShapeDtypeStruct((64, 1024), BF16),
            jax.ShapeDtypeStruct((32, 128), F32),
        ),
        in_specs=[hbm] * 5 + [smem] * 2,
        out_specs=(vmem, vmem),
        scratch_shapes=[
            V((8, 2048), BF16),
            V((1, 2048), F32),
            V((32, 128), BF16),
            V((64, 1024), BF16),
            V((1, 64), jnp.int32),
            V((4, 16, 256), BF16),
            V((4, 4, 2, 16, 256), BF16),
            V((2, 8, 32, 128), BF16),
            V((4, 4, 16, 128), BF16),
            V((4, 8, 16, 128), BF16),
            V((2, 16, 512), BF16),
            V((2, 4, 8, 16, 512), BF16),
            V((2, 8, 64, 512), BF16),
            V((8, 8, 128), jnp.int32),
            V((512, 512), BF16),
            V((4, 8, 16, 512), F32),
            V((4, 8, 16, 512), BF16),
            V((4, 8, 16, 512), BF16),
            V((4, 8, 16, 512), BF16),
            V((7, 4, 16, 128), BF16),
            V((3, 8, 16, 384), BF16),
            V((4, 16, 128), BF16),
            V((8, 16, 384), BF16),
            V((3, 16, 128), BF16),
            V((7, 16, 384), BF16),
            V((2, 16, 512), F32),
            V((8, 16, 128), BF16),
            V((4, 4, 16, 128), BF16),
            V((256, 512), BF16),
            V((2, 8, 32, 128), BF16),
            V((16, 32, 128), BF16),
            V((8, 2, 64, 512), BF16),
            V((2, 2, 32, 512), BF16),
            V((3, 2, 2, 64, 512), BF16),
            pltpu.SemaphoreType.DMA((N_SEM,)),
            pltpu.SemaphoreType.DMA((N_SEM,)),
            pltpu.SemaphoreType.DMA((5,)),
        ],
        compiler_params=pltpu.CompilerParams(
            collective_id=0, has_side_effects=True, vmem_limit_bytes=63 * 2**20
        ),
    )(features, gain.reshape(1, 2048), weights, states, ids.reshape(1, 64), sharpness, offset)


def solution(mesh):
    in_specs = (
        P(("batch", "param"), None),
        P(),
        P("batch", "param"),
        P(("batch", "param"), None),
        P(("batch", "param")),
        P(),
        P(),
    )
    out_specs = (P(("batch", "param"), None), P("batch", "param"))
    return jax.shard_map(body, mesh=mesh, in_specs=in_specs, out_specs=out_specs, check_vma=False)
```

```python
import jax
import jax.numpy as jnp
from jax import lax
from jax.experimental import pallas as pl
from jax.experimental.pallas import tpu as pltpu
from jax.sharding import PartitionSpec as P

F32 = jnp.float32
BF16 = jnp.bfloat16
MESH = pl.DeviceIdType.MESH
NX, NY, NZ = 4, 8, 8
N_SEM = 208
FAR_Y = (4, 3, 5, 2, 6, 1, 7)
FAR_X = (2, 1, 3)


def dot(a, b, contract=((1,), (0,))):
    return lax.dot_general(a, b, (contract, ((), ())), preferred_element_type=F32)


def kernel(
    feat_in, gain_in, wblk_in, src_in, idrow_in, sharp, shift,
    sg_out, hg_out,
    feat, gain, wblk, src, idrow, nsend, nq, wq, rpart, rbuf, gown, gbuf, sbuf, idbuf, pt,
    uown, usend, urecv, ub, ua1, ub1, ta, tb, ua2, ub2, xbuf,
    rgb, rgr, nt_buf, hq, hsum,
    spbuf, shalf, srecv, send_sem, recv_sem, in_sem,
):
    b = lax.axis_index("batch")
    p = lax.axis_index("param")
    zlo = b // 32
    x = lax.rem(b // 8, NX)
    y = lax.rem(b, NY)
    zhi = p // 2
    core = lax.rem(p, 2)
    z = zhi * 2 + zlo
    zp = z + 1 - 2 * zlo

    def dev(x=x, y=y, z=z, core=core):
        return (lax.rem(z, 2) * 32 + x * 8 + y, (z // 2) * 2 + core)

    def xd(d):
        return lax.rem(x + d, NX)

    def yd(d):
        return lax.rem(y + d, NY)

    def zd(d):
        return lax.rem(z + d, NZ)

    loads = [
        pltpu.make_async_copy(a, c, in_sem.at[i])
        for i, (a, c) in enumerate(
            ((wblk_in, wblk), (feat_in, feat), (gain_in, gain), (src_in, src), (idrow_in, idrow))
        )
    ]
    for load in loads:
        load.start()

    peers = [dev(y=yd(d)) for d in range(1, NY)]
    peers += [dev(y=yd(d), z=zp) for d in range(1, NY)]
    peers += [dev(z=zd(d)) for d in range(1, NZ)]
    peers += [dev(x=xd(d), z=zd(e)) for d in (1, 2, 3) for e in (0, 2, 4, 6)]
    peers += [dev(x=xd(d), z=zd(e), core=1 - core) for d in (0, 1, 2, 3) for e in (0, 2, 4, 6)]
    barrier = pltpu.get_barrier_semaphore()
    for peer in peers:
        pl.semaphore_signal(barrier, inc=1, device_id=peer, device_id_type=MESH)

    for load in loads[:3]:
        load.wait()
    f = feat[...].astype(F32)
    nf = f * lax.rsqrt(jnp.mean(f * f, axis=1, keepdims=True) + 1e-6) * gain[...]
    n16 = jnp.concatenate([nf[:, :1024], nf[:, 1024:]], axis=0).astype(BF16)
    for k in range(NX):
        nsend[k] = n16[:, k * 256:(k + 1) * 256]
    nq[x, zhi, core] = nsend[x]
    wq[zlo, y] = wblk[...]
    pl.semaphore_wait(barrier, len(peers))

    started = []

    def cp(a, c, device):
        i = len(started)
        copy = pltpu.make_async_remote_copy(
            src_ref=a, dst_ref=c, send_sem=send_sem.at[i], recv_sem=recv_sem.at[i],
            device_id=device, device_id_type=MESH,
        )
        copy.start()
        started.append(copy)
        return copy

    def arrived(copies):
        for copy in copies:
            copy.wait_recv()

    def over_x(src_of, dst_of):
        return [cp(src_of(xd(d)), dst_of(d), dev(x=xd(d))) for d in FAR_X]

    def over_y(src_of, dst_of):
        return [cp(src_of(yd(d)), dst_of(d), dev(y=yd(d))) for d in FAR_Y]

    def over_zy(src_of, dst_of):
        return [
            cp(src_of(f, yd(d)), dst_of(NY * f + d), dev(y=yd(d), z=zp if f else z))
            for d in FAR_Y + (0,) for f in (1, 0) if f or d
        ]

    XZ = [(d, e) for e in (4, 2, 6, 0) for d in FAR_X + (0,)]
    own_w = wq.at[zlo, y]
    w1 = over_zy(lambda f, t: own_w, lambda i: own_w)
    c_n = [
        cp(nsend.at[xd(d)], nq.at[x, zhi, core], dev(x=xd(d), z=zd(e)))
        for d, e in XZ if d or e
    ]

    for load in loads[3:]:
        load.wait()
    lane = lax.broadcasted_iota(jnp.int32, (8, 128), 1)
    twice = jnp.broadcast_to(jnp.concatenate([idrow[...], idrow[...]], axis=1), (8, 128))
    idbuf[z] = jnp.where(lane // 64 == zlo, twice, 0)
    s_f = src[...].astype(F32)
    s_scale = lax.rsqrt(jnp.sum(s_f * s_f, axis=1, keepdims=True) + 1e-6)
    s_unit = (s_f * s_scale).astype(BF16)
    sbuf[0, z] = s_unit[:, :512]
    sbuf[1, z] = s_unit[:, 512:]

    def hop(block, rows, step):
        ref = sbuf.at[:, block, rows]
        return cp(ref, ref, dev(z=zd(step)))

    every, low, high = pl.ds(0, 64), pl.ds(0, 32), pl.ds(32, 32)
    s_up, s_down = hop(z, every, 1), hop(z, every, 7)
    c_id = [cp(idbuf.at[z], idbuf.at[z], dev(z=zd(d))) for d in range(1, NZ)]

    arrived(c_n)
    c_ns = cp(nq.at[:, :, core], nq.at[:, :, core], dev(core=1 - core))
    arrived(w1)
    c_ns.wait_recv()

    halves = jnp.concatenate([wq[0].reshape(256, 128), wq[1].reshape(256, 128)], axis=1)
    both = dot(nq[...].reshape(512, 256), halves).reshape(32, 16, 256)
    rpart[...] = (both[:, 0:8, :128] + both[:, 8:16, 128:]).reshape(4, 4, 16, 128).astype(BF16)
    c_r = [
        cp(
            rpart.at[xd(d), zd(e) // 2], rbuf.at[x, p],
            dev(x=xd(d), z=zd(e), core=1 - core if flip else core),
        )
        for d, e in XZ for flip in (1, 0) if d or e or flip
    ]
    rbuf[x, p] = rpart[x, zhi]
    s_up.wait_recv()
    s_down.wait_recv()
    s_up, s_down = hop(zd(7), every, 1), hop(zd(1), every, 7)
    nt_buf[...] = nq[...].reshape(512, 256).T
    arrived(c_r)

    raw = jnp.sum(rbuf[...].astype(F32), axis=0).astype(BF16)
    raw_f = jnp.concatenate([raw[k] for k in range(8)], axis=1).astype(F32)
    g_scale = lax.rsqrt(jnp.sum(raw_f * raw_f, axis=1, keepdims=True) + 1e-6)
    g_unit = (raw_f * g_scale).astype(BF16)
    gown[0] = g_unit[:, :512]
    gown[1] = g_unit[:, 512:]
    gbuf[core, x, y] = gown[core]
    ga, gb = pl.ds(0, 128), pl.ds(128, 384)
    g1a = over_x(lambda t: gbuf.at[core, x, y, :, ga], lambda d: gbuf.at[core, x, y, :, ga])
    g1b = over_y(lambda t: gbuf.at[core, x, y, :, gb], lambda d: gbuf.at[core, x, y, :, gb])
    s_up.wait_recv()
    s_down.wait_recv()
    s_up, s_down = hop(zd(6), every, 1), hop(zd(2), every, 7)
    arrived(g1a)
    g2a = over_y(lambda t: gbuf.at[core, :, y, :, ga], lambda d: gbuf.at[core, :, y, :, ga])
    arrived(g1b)
    mine = gbuf.at[core, x, :, :, gb]
    g2b = {d: cp(mine, mine, dev(x=xd(d))) for d in FAR_X}
    s_up.wait_recv()
    s_down.wait_recv()
    s_up, s_down = hop(zd(5), low, 1), hop(zd(3), high, 7)
    arrived(g2a)

    sibling = dev(core=1 - core)
    c_g, c_u, u1b = {}, {}, []

    def share(d):
        if d:
            g2b[NX - d].wait_recv()
        block = gbuf.at[core, xd(d)]
        c_g[d] = cp(block, block, sibling)

    def weigh(d):
        k = xd(d)
        c_g[d].wait_recv()
        nt = ((1,), (1,))
        sim = dot(gbuf[0, k].reshape(128, 512), sbuf[0].reshape(512, 512), nt)
        sim += dot(gbuf[1, k].reshape(128, 512), sbuf[1].reshape(512, 512), nt)
        logits = scale * sim + offset
        goal = (zlo * 32 + k * 8 + row // 16) * 64 + zhi * 16 + lax.rem(row, 16)
        sign = jnp.where(goal == ids, 1.0, -1.0).astype(F32)
        weight = (-scale * sign / (1.0 + jnp.exp(sign * logits))).astype(BF16)
        pt[pl.ds(pl.multiple_of(k * 128, 128), 128), :] = weight
        usend[k] = dot(weight, sbuf[1 - core].reshape(512, 512)).reshape(8, 16, 512).astype(BF16)
        c_u[d] = cp(usend.at[k], urecv.at[k], sibling)
        uown[k] = dot(weight, sbuf[core].reshape(512, 512)).reshape(8, 16, 512)

    def pass_on(d):
        k = xd(d)
        c_u[d].wait_recv()
        ub[k] = (uown[k] + urecv[k].astype(F32)).astype(BF16)
        if d:
            u1b.append(cp(ub.at[k, :, :, gb], ub1.at[d - 1], dev(x=k)))

    share(0)
    scale, offset = sharp[0], shift[0]
    row = lax.broadcasted_iota(jnp.int32, (128, 1), 0)
    arrived(c_id)
    ids = jnp.concatenate(
        [idbuf[2 * q, 0:1] + idbuf[2 * q + 1, 0:1] for q in range(4)], axis=1
    )
    s_up.wait_recv()
    s_down.wait_recv()
    share(1)
    weigh(0)
    share(3)
    weigh(1)
    pass_on(0)
    share(2)
    weigh(3)
    pass_on(1)
    weigh(2)
    pass_on(3)
    pass_on(2)
    u1a = over_y(lambda t: ub.at[:, t, :, ga], lambda d: ua1.at[d - 1])

    for q in range(4):
        lhs = pt[:, q * 128:(q + 1) * 128]
        for h in range(2):
            part = dot(lhs, gbuf[h].reshape(512, 512), ((0,), (0,)))
            spbuf[2 * q:2 * q + 2, h] = part.reshape(2, 64, 512).astype(BF16)

    low32, high32 = pl.ds(0, 32), pl.ds(32, 32)
    r_up = cp(spbuf.at[zd(4), :, low32], shalf.at[0], dev(z=zd(1)))
    r_down = cp(spbuf.at[zd(4), :, high32], shalf.at[1], dev(z=zd(7)))

    def relay(step, r_up, r_down):
        r_up.wait_recv()
        r_down.wait_recv()
        up, down = zd(4 - step), zd(4 + step)
        if step == 1:
            spbuf[up, :, 0:32] = (spbuf[up, :, 0:32].astype(F32) + shalf[0].astype(F32)).astype(BF16)
            spbuf[down, :, 32:64] = (spbuf[down, :, 32:64].astype(F32) + shalf[1].astype(F32)).astype(BF16)
        else:
            spbuf[up] = (spbuf[up].astype(F32) + srecv[step - 2, 0].astype(F32)).astype(BF16)
            spbuf[down] = (spbuf[down].astype(F32) + srecv[step - 2, 1].astype(F32)).astype(BF16)
        return (
            cp(spbuf.at[up], srecv.at[step - 1, 0], dev(z=zd(1))),
            cp(spbuf.at[down], srecv.at[step - 1, 1], dev(z=zd(7))),
        )

    arrived(u1a)
    ta[...] = (ub[:, y, :, 0:128].astype(F32) + jnp.sum(ua1[...].astype(F32), axis=0)).astype(BF16)
    u2a = over_x(lambda t: ta.at[t], lambda d: ua2.at[d - 1])
    arrived(u1b)
    tb[...] = (ub[x, :, :, 128:512].astype(F32) + jnp.sum(ub1[...].astype(F32), axis=0)).astype(BF16)
    u2b = over_y(lambda t: tb.at[t], lambda d: ub2.at[d - 1])
    r_up, r_down = relay(1, r_up, r_down)
    arrived(u2a)
    xbuf[core, :, 0:128] = ta[x].astype(F32) + jnp.sum(ua2[...].astype(F32), axis=0)
    arrived(u2b)
    xbuf[core, :, 128:512] = tb[y].astype(F32) + jnp.sum(ub2[...].astype(F32), axis=0)
    c_x = cp(xbuf.at[core], xbuf.at[core], dev(core=1 - core))
    c_x.wait_recv()

    u = jnp.concatenate([xbuf[0], xbuf[1]], axis=1)
    g_f = raw_f * g_scale
    inner = jnp.sum(g_f * u, axis=1, keepdims=True)
    raw_grad = (g_scale * (u - g_f * inner)).astype(BF16)
    for k in range(8):
        rgb[k] = raw_grad[:, k * 128:(k + 1) * 128]
    rgr[x, zhi] = rgb[p]
    c_rg = [
        cp(rgb.at[(zd(e) // 2) * 2 + core], rgr.at[x, zhi], dev(x=xd(d), z=zd(e)))
        for d, e in XZ if d or e
    ]
    r_up, r_down = relay(2, r_up, r_down)
    arrived(c_rg)
    rg = rgr[...].astype(F32).reshape(32, 8, 128)
    zero = jnp.zeros((32, 8, 128), F32)
    rg_top = jnp.concatenate([rg, zero], axis=1).reshape(512, 128).astype(BF16)
    rg_bottom = jnp.concatenate([zero, rg], axis=1).reshape(512, 128).astype(BF16)
    part = dot(nt_buf[...], jnp.concatenate([rg_top, rg_bottom], axis=1)).astype(BF16)
    hq[0] = part[:, :128].reshape(8, 32, 128)
    hq[1] = part[:, 128:].reshape(8, 32, 128)
    c_h = over_zy(lambda f, t: hq.at[1 - zlo if f else zlo, t], lambda i: hsum.at[i])
    hsum[0] = hq[zlo, y]
    r_up, r_down = relay(3, r_up, r_down)

    r_up.wait_recv()
    r_down.wait_recv()
    su_f = s_f * s_scale
    sums = spbuf[z].astype(F32) + srecv[2, 0].astype(F32) + srecv[2, 1].astype(F32)
    usg = jnp.concatenate([sums[0], sums[1]], axis=1)
    inner_s = jnp.sum(su_f * usg, axis=1, keepdims=True)
    sg_out[...] = (s_scale * (usg - su_f * inner_s)).astype(BF16)

    arrived(c_h)
    hg_out[...] = jnp.sum(hsum[...].astype(F32), axis=0)
    for copy in started:
        copy.wait_send()


def copy_out(sg_in, hg_in, sg_out, hg_out):
    sg_out[...] = sg_in[...]
    hg_out[...] = hg_in[...]


def body(features, gain, weights, states, ids, sharpness, offset):
    vmem = pl.BlockSpec(memory_space=pltpu.VMEM)
    hbm = pl.BlockSpec(memory_space=pltpu.HBM)
    smem = pl.BlockSpec(memory_space=pltpu.SMEM)
    V = pltpu.VMEM
    sg, hg = pl.pallas_call(
        kernel,
        out_shape=(
            jax.ShapeDtypeStruct((64, 1024), BF16),
            jax.ShapeDtypeStruct((32, 128), F32),
        ),
        in_specs=[hbm] * 5 + [smem] * 2,
        out_specs=(vmem, vmem),
        scratch_shapes=[
            V((8, 2048), BF16),
            V((1, 2048), F32),
            V((32, 128), BF16),
            V((64, 1024), BF16),
            V((1, 64), jnp.int32),
            V((4, 16, 256), BF16),
            V((4, 4, 2, 16, 256), BF16),
            V((2, 8, 32, 128), BF16),
            V((4, 4, 16, 128), BF16),
            V((4, 8, 16, 128), BF16),
            V((2, 16, 512), BF16),
            V((2, 4, 8, 16, 512), BF16),
            V((2, 8, 64, 512), BF16),
            V((8, 8, 128), jnp.int32),
            V((512, 512), BF16),
            V((4, 8, 16, 512), F32),
            V((4, 8, 16, 512), BF16),
            V((4, 8, 16, 512), BF16),
            V((4, 8, 16, 512), BF16),
            V((7, 4, 16, 128), BF16),
            V((3, 8, 16, 384), BF16),
            V((4, 16, 128), BF16),
            V((8, 16, 384), BF16),
            V((3, 16, 128), BF16),
            V((7, 16, 384), BF16),
            V((2, 16, 512), F32),
            V((8, 16, 128), BF16),
            V((4, 4, 16, 128), BF16),
            V((256, 512), BF16),
            V((2, 8, 32, 128), BF16),
            V((16, 32, 128), BF16),
            V((8, 2, 64, 512), BF16),
            V((2, 2, 32, 512), BF16),
            V((3, 2, 2, 64, 512), BF16),
            pltpu.SemaphoreType.DMA((N_SEM,)),
            pltpu.SemaphoreType.DMA((N_SEM,)),
            pltpu.SemaphoreType.DMA((5,)),
        ],
        compiler_params=pltpu.CompilerParams(
            collective_id=0, has_side_effects=True, vmem_limit_bytes=63 * 2**20
        ),
    )(features, gain.reshape(1, 2048), weights, states, ids.reshape(1, 64), sharpness, offset)
    return pl.pallas_call(
        copy_out,
        out_shape=(
            jax.ShapeDtypeStruct((64, 1024), BF16),
            jax.ShapeDtypeStruct((32, 128), F32),
        ),
        in_specs=[vmem] * 2,
        out_specs=(vmem, vmem),
    )(sg, hg)


def solution(mesh):
    in_specs = (
        P(("batch", "param"), None),
        P(),
        P("batch", "param"),
        P(("batch", "param"), None),
        P(("batch", "param")),
        P(),
        P(),
    )
    out_specs = (P(("batch", "param"), None), P("batch", "param"))
    return jax.shard_map(body, mesh=mesh, in_specs=in_specs, out_specs=out_specs, check_vma=False)
```

```python
import jax
import jax.numpy as jnp
from jax import lax
from jax.experimental import pallas as pl
from jax.experimental.pallas import tpu as pltpu
from jax.sharding import PartitionSpec as P

F32 = jnp.float32
BF16 = jnp.bfloat16
MESH = pl.DeviceIdType.MESH
NX, NY, NZ = 4, 8, 8
N_SEM = 208
FAR_Y = (4, 3, 5, 2, 6, 1, 7)
FAR_X = (2, 1, 3)


def dot(a, b, contract=((1,), (0,))):
    return lax.dot_general(a, b, (contract, ((), ())), preferred_element_type=F32)


def kernel(
    feat_in, gain_in, wblk_in, src_in, idrow_in, sharp, shift,
    sg_out, hg_out,
    feat, gain, wblk, src, idrow, nsend, nq, wq, rpart, rbuf, gown, gbuf, sbuf, idbuf, pt,
    uown, usend, urecv, ub, ua1, ub1, ta, tb, ua2, ub2, xbuf,
    rgb, rgr, nt_buf, hq, hsum,
    spbuf, shalf, srecv, send_sem, recv_sem, in_sem,
):
    b = lax.axis_index("batch")
    p = lax.axis_index("param")
    zlo = b // 32
    x = lax.rem(b // 8, NX)
    y = lax.rem(b, NY)
    zhi = p // 2
    core = lax.rem(p, 2)
    z = zhi * 2 + zlo
    zp = z + 1 - 2 * zlo

    def dev(x=x, y=y, z=z, core=core):
        return (lax.rem(z, 2) * 32 + x * 8 + y, (z // 2) * 2 + core)

    def xd(d):
        return lax.rem(x + d, NX)

    def yd(d):
        return lax.rem(y + d, NY)

    def zd(d):
        return lax.rem(z + d, NZ)

    peers = [dev(x=xd(d), z=zd(e), core=1 - core) for e in (4, 2, 6, 0) for d in (2, 1, 3, 0)]
    peers += [dev(x=xd(d), z=zd(e)) for e in (4, 2, 6, 0) for d in (2, 1, 3)]
    peers += [dev(y=yd(d), z=zp) for d in FAR_Y]
    peers += [dev(y=yd(d)) for d in FAR_Y]
    peers += [dev(z=zd(d)) for d in FAR_Y]
    barrier = pltpu.get_barrier_semaphore()
    for peer in peers:
        pl.semaphore_signal(barrier, inc=1, device_id=peer, device_id_type=MESH)

    loads = [
        pltpu.make_async_copy(a, c, in_sem.at[i])
        for i, (a, c) in enumerate(
            ((wblk_in, wblk), (feat_in, feat), (gain_in, gain), (src_in, src), (idrow_in, idrow))
        )
    ]
    for load in loads:
        load.start()

    for load in loads[:3]:
        load.wait()
    f = feat[...].astype(F32)
    nf = f * lax.rsqrt(jnp.mean(f * f, axis=1, keepdims=True) + 1e-6) * gain[...]
    n16 = jnp.concatenate([nf[:, :1024], nf[:, 1024:]], axis=0).astype(BF16)
    for k in range(NX):
        nsend[k] = n16[:, k * 256:(k + 1) * 256]
    nq[x, zhi, core] = nsend[x]
    wq[zlo, y] = wblk[...]
    pl.semaphore_wait(barrier, len(peers))

    started = []

    def cp(a, c, device):
        i = len(started)
        copy = pltpu.make_async_remote_copy(
            src_ref=a, dst_ref=c, send_sem=send_sem.at[i], recv_sem=recv_sem.at[i],
            device_id=device, device_id_type=MESH,
        )
        copy.start()
        started.append(copy)
        return copy

    def arrived(copies):
        for copy in copies:
            copy.wait_recv()

    def over_x(src_of, dst_of):
        return [cp(src_of(xd(d)), dst_of(d), dev(x=xd(d))) for d in FAR_X]

    def over_y(src_of, dst_of):
        return [cp(src_of(yd(d)), dst_of(d), dev(y=yd(d))) for d in FAR_Y]

    def over_zy(src_of, dst_of):
        return [
            cp(src_of(f, yd(d)), dst_of(NY * f + d), dev(y=yd(d), z=zp if f else z))
            for d in FAR_Y + (0,) for f in (1, 0) if f or d
        ]

    XZ = [(d, e) for e in (4, 2, 6, 0) for d in FAR_X + (0,)]
    own_w = wq.at[zlo, y]
    c_n = [
        cp(nsend.at[xd(d)], nq.at[x, zhi, core], dev(x=xd(d), z=zd(e)))
        for d, e in XZ if d or e
    ]
    w1 = over_zy(lambda f, t: own_w, lambda i: own_w)

    for load in loads[3:]:
        load.wait()
    lane = lax.broadcasted_iota(jnp.int32, (8, 128), 1)
    twice = jnp.broadcast_to(jnp.concatenate([idrow[...], idrow[...]], axis=1), (8, 128))
    idbuf[z] = jnp.where(lane // 64 == zlo, twice, 0)
    s_f = src[...].astype(F32)
    s_scale = lax.rsqrt(jnp.sum(s_f * s_f, axis=1, keepdims=True) + 1e-6)
    s_unit = (s_f * s_scale).astype(BF16)
    sbuf[0, z] = s_unit[:, :512]
    sbuf[1, z] = s_unit[:, 512:]

    def hop(block, rows, step):
        ref = sbuf.at[:, block, rows]
        return cp(ref, ref, dev(z=zd(step)))

    every, low, high = pl.ds(0, 64), pl.ds(0, 32), pl.ds(32, 32)
    s_up, s_down = hop(z, every, 1), hop(z, every, 7)
    c_id = [cp(idbuf.at[z], idbuf.at[z], dev(z=zd(d))) for d in range(1, NZ)]

    arrived(c_n)
    c_ns = cp(nq.at[:, :, core], nq.at[:, :, core], dev(core=1 - core))
    arrived(w1)
    c_ns.wait_recv()

    halves = jnp.concatenate([wq[0].reshape(256, 128), wq[1].reshape(256, 128)], axis=1)
    both = dot(nq[...].reshape(512, 256), halves).reshape(32, 16, 256)
    rpart[...] = (both[:, 0:8, :128] + both[:, 8:16, 128:]).reshape(4, 4, 16, 128).astype(BF16)
    c_r = [
        cp(
            rpart.at[xd(d), zd(e) // 2], rbuf.at[x, p],
            dev(x=xd(d), z=zd(e), core=1 - core if flip else core),
        )
        for d, e in XZ for flip in (1, 0) if d or e or flip
    ]
    rbuf[x, p] = rpart[x, zhi]
    s_up.wait_recv()
    s_down.wait_recv()
    s_up, s_down = hop(zd(7), every, 1), hop(zd(1), every, 7)
    nt_buf[...] = nq[...].reshape(512, 256).T
    arrived(c_r)

    raw = jnp.sum(rbuf[...].astype(F32), axis=0).astype(BF16)
    raw_f = jnp.concatenate([raw[k] for k in range(8)], axis=1).astype(F32)
    g_scale = lax.rsqrt(jnp.sum(raw_f * raw_f, axis=1, keepdims=True) + 1e-6)
    g_unit = (raw_f * g_scale).astype(BF16)
    gown[0] = g_unit[:, :512]
    gown[1] = g_unit[:, 512:]
    gbuf[core, x, y] = gown[core]
    ga, gb = pl.ds(0, 128), pl.ds(128, 384)
    g1a = over_x(lambda t: gbuf.at[core, x, y, :, ga], lambda d: gbuf.at[core, x, y, :, ga])
    g1b = over_y(lambda t: gbuf.at[core, x, y, :, gb], lambda d: gbuf.at[core, x, y, :, gb])
    s_up.wait_recv()
    s_down.wait_recv()
    s_up, s_down = hop(zd(6), every, 1), hop(zd(2), every, 7)
    arrived(g1a)
    g2a = over_y(lambda t: gbuf.at[core, :, y, :, ga], lambda d: gbuf.at[core, :, y, :, ga])
    arrived(g1b)
    mine = gbuf.at[core, x, :, :, gb]
    g2b = {d: cp(mine, mine, dev(x=xd(d))) for d in FAR_X}
    s_up.wait_recv()
    s_down.wait_recv()
    s_up, s_down = hop(zd(5), low, 1), hop(zd(3), high, 7)
    arrived(g2a)

    sibling = dev(core=1 - core)
    c_g, c_u, u1b = {}, {}, []

    def share(d):
        if d:
            g2b[NX - d].wait_recv()
        block = gbuf.at[core, xd(d)]
        c_g[d] = cp(block, block, sibling)

    def weigh(d):
        k = xd(d)
        c_g[d].wait_recv()
        nt = ((1,), (1,))
        sim = dot(gbuf[0, k].reshape(128, 512), sbuf[0].reshape(512, 512), nt)
        sim += dot(gbuf[1, k].reshape(128, 512), sbuf[1].reshape(512, 512), nt)
        logits = scale * sim + offset
        goal = (zlo * 32 + k * 8 + row // 16) * 64 + zhi * 16 + lax.rem(row, 16)
        sign = jnp.where(goal == ids, 1.0, -1.0).astype(F32)
        weight = (-scale * sign / (1.0 + jnp.exp(sign * logits))).astype(BF16)
        pt[pl.ds(pl.multiple_of(k * 128, 128), 128), :] = weight
        usend[k] = dot(weight, sbuf[1 - core].reshape(512, 512)).reshape(8, 16, 512).astype(BF16)
        c_u[d] = cp(usend.at[k], urecv.at[k], sibling)
        uown[k] = dot(weight, sbuf[core].reshape(512, 512)).reshape(8, 16, 512)

    def pass_on(d):
        k = xd(d)
        c_u[d].wait_recv()
        ub[k] = (uown[k] + urecv[k].astype(F32)).astype(BF16)
        if d:
            u1b.append(cp(ub.at[k, :, :, gb], ub1.at[d - 1], dev(x=k)))

    share(0)
    scale, offset = sharp[0], shift[0]
    row = lax.broadcasted_iota(jnp.int32, (128, 1), 0)
    arrived(c_id)
    ids = jnp.concatenate(
        [idbuf[2 * q, 0:1] + idbuf[2 * q + 1, 0:1] for q in range(4)], axis=1
    )
    s_up.wait_recv()
    s_down.wait_recv()
    share(1)
    weigh(0)
    share(3)
    weigh(1)
    pass_on(0)
    share(2)
    weigh(3)
    pass_on(1)
    weigh(2)
    pass_on(3)
    pass_on(2)
    u1a = over_y(lambda t: ub.at[:, t, :, ga], lambda d: ua1.at[d - 1])

    for q in range(4):
        lhs = pt[:, q * 128:(q + 1) * 128]
        for h in range(2):
            part = dot(lhs, gbuf[h].reshape(512, 512), ((0,), (0,)))
            spbuf[2 * q:2 * q + 2, h] = part.reshape(2, 64, 512).astype(BF16)

    low32, high32 = pl.ds(0, 32), pl.ds(32, 32)
    r_up = cp(spbuf.at[zd(4), :, low32], shalf.at[0], dev(z=zd(1)))
    r_down = cp(spbuf.at[zd(4), :, high32], shalf.at[1], dev(z=zd(7)))

    def relay(step, r_up, r_down):
        r_up.wait_recv()
        r_down.wait_recv()
        up, down = zd(4 - step), zd(4 + step)
        if step == 1:
            spbuf[up, :, 0:32] = (spbuf[up, :, 0:32].astype(F32) + shalf[0].astype(F32)).astype(BF16)
            spbuf[down, :, 32:64] = (spbuf[down, :, 32:64].astype(F32) + shalf[1].astype(F32)).astype(BF16)
        else:
            spbuf[up] = (spbuf[up].astype(F32) + srecv[step - 2, 0].astype(F32)).astype(BF16)
            spbuf[down] = (spbuf[down].astype(F32) + srecv[step - 2, 1].astype(F32)).astype(BF16)
        return (
            cp(spbuf.at[up], srecv.at[step - 1, 0], dev(z=zd(1))),
            cp(spbuf.at[down], srecv.at[step - 1, 1], dev(z=zd(7))),
        )

    arrived(u1a)
    ta[...] = (ub[:, y, :, 0:128].astype(F32) + jnp.sum(ua1[...].astype(F32), axis=0)).astype(BF16)
    u2a = over_x(lambda t: ta.at[t], lambda d: ua2.at[d - 1])
    arrived(u1b)
    tb[...] = (ub[x, :, :, 128:512].astype(F32) + jnp.sum(ub1[...].astype(F32), axis=0)).astype(BF16)
    u2b = over_y(lambda t: tb.at[t], lambda d: ub2.at[d - 1])
    r_up, r_down = relay(1, r_up, r_down)
    arrived(u2a)
    xbuf[core, :, 0:128] = ta[x].astype(F32) + jnp.sum(ua2[...].astype(F32), axis=0)
    arrived(u2b)
    xbuf[core, :, 128:512] = tb[y].astype(F32) + jnp.sum(ub2[...].astype(F32), axis=0)
    c_x = cp(xbuf.at[core], xbuf.at[core], dev(core=1 - core))
    c_x.wait_recv()

    u = jnp.concatenate([xbuf[0], xbuf[1]], axis=1)
    g_f = raw_f * g_scale
    inner = jnp.sum(g_f * u, axis=1, keepdims=True)
    raw_grad = (g_scale * (u - g_f * inner)).astype(BF16)
    for k in range(8):
        rgb[k] = raw_grad[:, k * 128:(k + 1) * 128]
    rgr[x, zhi] = rgb[p]
    c_rg = [
        cp(rgb.at[(zd(e) // 2) * 2 + core], rgr.at[x, zhi], dev(x=xd(d), z=zd(e)))
        for d, e in XZ if d or e
    ]
    r_up, r_down = relay(2, r_up, r_down)
    arrived(c_rg)
    rg = rgr[...].astype(F32).reshape(32, 8, 128)
    zero = jnp.zeros((32, 8, 128), F32)
    rg_top = jnp.concatenate([rg, zero], axis=1).reshape(512, 128).astype(BF16)
    rg_bottom = jnp.concatenate([zero, rg], axis=1).reshape(512, 128).astype(BF16)
    part = dot(nt_buf[...], jnp.concatenate([rg_top, rg_bottom], axis=1)).astype(BF16)
    hq[0] = part[:, :128].reshape(8, 32, 128)
    hq[1] = part[:, 128:].reshape(8, 32, 128)
    c_h = over_zy(lambda f, t: hq.at[1 - zlo if f else zlo, t], lambda i: hsum.at[i])
    hsum[0] = hq[zlo, y]
    r_up, r_down = relay(3, r_up, r_down)

    r_up.wait_recv()
    r_down.wait_recv()
    su_f = s_f * s_scale
    sums = spbuf[z].astype(F32) + srecv[2, 0].astype(F32) + srecv[2, 1].astype(F32)
    usg = jnp.concatenate([sums[0], sums[1]], axis=1)
    inner_s = jnp.sum(su_f * usg, axis=1, keepdims=True)
    sg_out[...] = (s_scale * (usg - su_f * inner_s)).astype(BF16)

    arrived(c_h)
    hg_out[...] = jnp.sum(hsum[...].astype(F32), axis=0)
    for copy in started:
        copy.wait_send()


def copy_out(sg_in, hg_in, sg_out, hg_out):
    sg_out[...] = sg_in[...]
    hg_out[...] = hg_in[...]


def body(features, gain, weights, states, ids, sharpness, offset):
    vmem = pl.BlockSpec(memory_space=pltpu.VMEM)
    hbm = pl.BlockSpec(memory_space=pltpu.HBM)
    smem = pl.BlockSpec(memory_space=pltpu.SMEM)
    V = pltpu.VMEM
    sg, hg = pl.pallas_call(
        kernel,
        out_shape=(
            jax.ShapeDtypeStruct((64, 1024), BF16),
            jax.ShapeDtypeStruct((32, 128), F32),
        ),
        in_specs=[hbm] * 5 + [smem] * 2,
        out_specs=(vmem, vmem),
        scratch_shapes=[
            V((8, 2048), BF16),
            V((1, 2048), F32),
            V((32, 128), BF16),
            V((64, 1024), BF16),
            V((1, 64), jnp.int32),
            V((4, 16, 256), BF16),
            V((4, 4, 2, 16, 256), BF16),
            V((2, 8, 32, 128), BF16),
            V((4, 4, 16, 128), BF16),
            V((4, 8, 16, 128), BF16),
            V((2, 16, 512), BF16),
            V((2, 4, 8, 16, 512), BF16),
            V((2, 8, 64, 512), BF16),
            V((8, 8, 128), jnp.int32),
            V((512, 512), BF16),
            V((4, 8, 16, 512), F32),
            V((4, 8, 16, 512), BF16),
            V((4, 8, 16, 512), BF16),
            V((4, 8, 16, 512), BF16),
            V((7, 4, 16, 128), BF16),
            V((3, 8, 16, 384), BF16),
            V((4, 16, 128), BF16),
            V((8, 16, 384), BF16),
            V((3, 16, 128), BF16),
            V((7, 16, 384), BF16),
            V((2, 16, 512), F32),
            V((8, 16, 128), BF16),
            V((4, 4, 16, 128), BF16),
            V((256, 512), BF16),
            V((2, 8, 32, 128), BF16),
            V((16, 32, 128), BF16),
            V((8, 2, 64, 512), BF16),
            V((2, 2, 32, 512), BF16),
            V((3, 2, 2, 64, 512), BF16),
            pltpu.SemaphoreType.DMA((N_SEM,)),
            pltpu.SemaphoreType.DMA((N_SEM,)),
            pltpu.SemaphoreType.DMA((5,)),
        ],
        compiler_params=pltpu.CompilerParams(
            collective_id=0, has_side_effects=True, vmem_limit_bytes=63 * 2**20
        ),
    )(features, gain.reshape(1, 2048), weights, states, ids.reshape(1, 64), sharpness, offset)
    return pl.pallas_call(
        copy_out,
        out_shape=(
            jax.ShapeDtypeStruct((64, 1024), BF16),
            jax.ShapeDtypeStruct((32, 128), F32),
        ),
        in_specs=[vmem] * 2,
        out_specs=(vmem, vmem),
    )(sg, hg)


def solution(mesh):
    in_specs = (
        P(("batch", "param"), None),
        P(),
        P("batch", "param"),
        P(("batch", "param"), None),
        P(("batch", "param")),
        P(),
        P(),
    )
    out_specs = (P(("batch", "param"), None), P("batch", "param"))
    return jax.shard_map(body, mesh=mesh, in_specs=in_specs, out_specs=out_specs, check_vma=False)
```
